256 devices in a mesh: ctx: 32 (over y_lo, z, core), tp: 8 (over x, y_hi).
Axes of the slice: x: 4, y: 4 (y_hi: 2, y_lo: 2; y = y_hi * 2 + y_lo), z: 8, core: 2. Of those that a mesh axis runs over, the one named last changes fastest.
Arguments:
- queries: bfloat16 [24576, 64, 128], P('ctx', 'tp'), may hold values from -10 to 10
- key_rows: bfloat16 [24576, 8, 128], P('ctx', 'tp'), may hold values from -6 to 6
- value_rows: bfloat16 [24576, 8, 128], P('ctx', 'tp'), may hold values from -6 to 6
- doc_ids: int32 [24576], replicated, may hold values from 0 to 14, as said below
- plan: int32 [4, 32], P(None, 'ctx'), may hold values from -1 to 30, as said below
Outputs:
- attended: bfloat16 [64, 24576, 128], P(None, ('ctx', 'tp'))
The draws below stay inside these ranges and needn't reach their ends.
Inputs may be any that keep to these rules, and one draw needn't show every extreme that they name: `doc_ids`: Non-decreasing from 0 in steps of at most one; every document is a run of at most 3072 tokens, and one document has exactly 3072. plan[r, c] is c - 1 - r when some token of span c and some token of span c - 1 - r belong to one document, else -1.
All inputs are finite; a program needn't handle non-finite values.
Results may differ from the reference program's by a relative error of at most 0.0039.
Values may be sent and summed in bfloat16 or wider, within the bound.
A program may use at most 64 MiB of HBM per device.

```python
import jax
import jax.numpy as jnp
from jax import lax

HEADS = 64
KV_HEADS = 8
HEAD_DIM = 128
ROWS = 768
ROUNDS = 4
TOKENS = 24576
MAXDOC = 3072


def document_ids(key):
    half_doc = MAXDOC // 2
    slot_count = TOKENS // half_doc
    offsets = jax.random.randint(jax.random.fold_in(key, 601), (slot_count,), 0, half_doc)
    chosen = jax.random.randint(jax.random.fold_in(key, 602), (), 0, slot_count - 1)
    slot_ids = jnp.arange(slot_count, dtype=jnp.int32)
    fixed_start = (slot_ids == chosen) | (slot_ids == chosen + 2) | (slot_ids == 0) | (slot_ids == slot_count - 1)
    offsets = jnp.where(fixed_start, 0, offsets)
    present = (slot_ids != chosen + 1).astype(jnp.int32)
    places = slot_ids * half_doc + offsets
    starts = jnp.zeros((TOKENS,), jnp.int32).at[places].add(present)
    return (jnp.cumsum(starts) - starts[0]).astype(jnp.int32)


def draw_queries(key, part):
    key = jax.random.fold_in(key, 11)
    shape = (TOKENS, HEADS, HEAD_DIM)
    base = jax.random.truncated_normal(key, -6.0, 6.0, shape, jnp.float32)
    return base.astype(jnp.bfloat16)


def draw_key_rows(key, part):
    key = jax.random.fold_in(key, 12)
    shape = (TOKENS, KV_HEADS, HEAD_DIM)
    base = jax.random.truncated_normal(key, -6.0, 6.0, shape, jnp.float32)
    return base.astype(jnp.bfloat16)


def draw_doc_ids(key, part):
    found = document_ids(key)
    return found


def draw_plan(key, part):
    found = document_ids(key)
    span_count = TOKENS // ROWS
    span_ids = jnp.arange(span_count, dtype=jnp.int32)
    round_ids = jnp.arange(ROUNDS, dtype=jnp.int32)[:, None]
    partner = span_ids[None, :] - 1 - round_ids
    last_key = found[jnp.maximum(partner, 0) * ROWS + ROWS - 1]
    first_query = found[span_ids * ROWS][None, :]
    return jnp.where((partner >= 0) & (last_key == first_query), partner, -1).astype(jnp.int32)


def level_of(key, extent, shards, smallest, top_value):
    def one(axis_at, blocks):
        heights = jax.random.uniform(jax.random.fold_in(jax.random.fold_in(key, 6), axis_at), (blocks,), jnp.float32, smallest / len(shards), top_value / len(shards))
        return jnp.repeat(jnp.exp(heights), extent[axis_at] // blocks).reshape((-1,) + (1,) * (len(extent) - axis_at - 1))

    loudness = one(*shards[0])
    for cut in shards[1:]:
        loudness = loudness * one(*cut)
    return loudness


def noise(own_key, extent, scale, reach, shards=(), kind=jnp.bfloat16):
    level = level_of(own_key, extent, shards, -0.22, 0.18) if shards else 1.0
    array = jax.random.normal(own_key, extent, jnp.float32) * scale * level
    return jnp.minimum(jnp.maximum(array, -reach), reach).astype(kind)


def setup_inputs(seed: int = 0) -> dict:
    streams_of = jax.random.split(jax.random.key(seed), 6)
    queries = draw_queries(jax.random.fold_in(streams_of[5], 71), 0)
    key_rows = draw_key_rows(jax.random.fold_in(streams_of[5], 71), 0)
    value_rows = noise(streams_of[2], (TOKENS, KV_HEADS, HEAD_DIM), 1.0, 6.0, ((0, 32), (1, 8)))
    doc_ids = draw_doc_ids(jax.random.fold_in(streams_of[5], 71), 0)
    plan = draw_plan(jax.random.fold_in(streams_of[5], 71), 0)
    return dict(queries=queries, key_rows=key_rows, value_rows=value_rows, doc_ids=doc_ids, plan=plan)


def reference(queries, key_rows, value_rows, doc_ids, plan):
    head_group = HEADS // KV_HEADS
    score_scale = HEAD_DIM ** -0.5
    span_count = TOKENS // ROWS
    offsets = jnp.arange(ROWS, dtype=jnp.int32)

    def one_span(span):
        start = (span * ROWS).astype(jnp.int32)
        query_block = lax.dynamic_slice_in_dim(queries, start, ROWS, 0).astype(jnp.float32)
        query_docs = lax.dynamic_slice_in_dim(doc_ids, start, ROWS, 0)
        query_pos = start + offsets
        partners = [span.astype(jnp.int32)] + [plan[j, span] for j in range(ROUNDS)]
        key_list = []
        value_list = []
        mask_list = []
        for partner in partners:
            safe = (jnp.maximum(partner, 0) * ROWS).astype(jnp.int32)
            key_docs = lax.dynamic_slice_in_dim(doc_ids, safe, ROWS, 0)
            key_pos = safe + offsets
            mask_list.append((key_docs[None, :] == query_docs[:, None]) & (key_pos[None, :] <= query_pos[:, None]) & (partner >= 0))
            key_list.append(lax.dynamic_slice_in_dim(key_rows, safe, ROWS, 0))
            value_list.append(lax.dynamic_slice_in_dim(value_rows, safe, ROWS, 0))
        all_keys = jnp.concatenate(key_list, 0).astype(jnp.float32)
        all_values = jnp.concatenate(value_list, 0).astype(jnp.float32)
        all_mask = jnp.concatenate(mask_list, 1)
        grouped = query_block.reshape(ROWS, KV_HEADS, head_group, HEAD_DIM)
        scores = jnp.einsum('rkgd,skd->kgrs', grouped, all_keys) * score_scale
        scores = jnp.where(all_mask[None, None], scores, -jnp.inf)
        largest = jnp.max(scores, axis=-1, keepdims=True)
        weights = jnp.exp(scores - largest)
        total = jnp.sum(weights, axis=-1, keepdims=True)
        rounded = lax.optimization_barrier(weights.astype(jnp.bfloat16)).astype(jnp.float32)
        summed = jnp.einsum('kgrs,skd->kgrd', rounded, all_values)
        result = (summed / total).astype(jnp.bfloat16)
        return result.reshape(HEADS, ROWS, HEAD_DIM)

    blocks = lax.map(one_span, jnp.arange(span_count, dtype=jnp.int32))
    return blocks.transpose(1, 0, 2, 3).reshape(HEADS, TOKENS, HEAD_DIM)
```

```python
import functools

import jax
import jax.numpy as jnp
from jax import lax
from jax.experimental import pallas as pl
from jax.experimental.pallas import tpu as pltpu
from jax.sharding import PartitionSpec as P

MESH = pl.DeviceIdType.MESH
FAR = -1e30
TILE = 256
LANES = 128


def kernel(exponent, q_ref, own_ref, docs_ref, out_ref, kv, key_marks, query_marks, scores, peaks, running,
           finished, outgoing, kv_send, kv_recv, out_send, out_recv, own_sem):
    rows = own_ref.shape[1]
    tp_size = outgoing.shape[0]
    heads = outgoing.shape[1]
    chunk = outgoing.shape[2]
    block = chunk * heads
    spans = lax.axis_size("ctx")
    half = rows // 2
    doc_rows = rows // LANES
    tiles = rows // TILE
    span = lax.axis_index("ctx")
    head_place = lax.axis_index("tp")
    core = lax.rem(span, 2)
    mate = span + 1 - 2 * core
    ahead = lax.rem(span + 2, spans)
    behind = lax.rem(span + spans - 2, spans)

    barrier = pltpu.get_barrier_semaphore()
    for other in (mate, ahead, behind):
        pl.semaphore_signal(barrier, inc=1, device_id=(other, head_place), device_id_type=MESH)
    for step in range(1, tp_size):
        pl.semaphore_signal(
            barrier, inc=1, device_id=(span, lax.rem(head_place + step, tp_size)), device_id_type=MESH
        )
    pl.semaphore_wait(barrier, tp_size + 2)

    def piece(ref, part):
        return ref.at[:, pl.ds((1 - part) * half, half)]

    def hop(source, slot, kind, part, device):
        return pltpu.make_async_remote_copy(
            src_ref=piece(source, part),
            dst_ref=piece(kv.at[slot], part),
            send_sem=kv_send.at[kind, part],
            recv_sem=kv_recv.at[slot, part],
            device_id=(device, head_place),
            device_id_type=MESH,
        )

    def landed(slot, part):
        hop(own_ref, slot, 0, part, mate).wait_recv()

    for part in range(2):
        hop(own_ref, 1, 1, part, ahead).start()

    @pl.when(core == 0)
    def _():
        for part in range(2):
            hop(own_ref, 0, 0, part, mate).start()

    def mark(step, carry):
        for back in range(5):
            place = lax.rem(span + spans - back, spans) * doc_rows + step
            docs = docs_ref[pl.ds(place, 1), :]
            hit = lax.broadcasted_iota(jnp.int32, (LANES, LANES), 0) == docs
            turned = jnp.where(hit, 1.0, 0.0).astype(jnp.float32).T
            at = pl.multiple_of(step * LANES, LANES)
            key_marks[back, pl.ds(at, LANES), :] = turned.astype(jnp.bfloat16)
            if back == 0:
                miss = (1.0 - turned) * FAR
                wide = jnp.broadcast_to(miss[:, None, :], (LANES, heads, LANES)).reshape(LANES * heads, LANES)
                at = pl.multiple_of(step * LANES * heads, LANES * heads)
                query_marks[pl.ds(at, LANES * heads), :] = wide.astype(jnp.bfloat16)
        return carry

    lax.fori_loop(0, doc_rows, mark, 0)

    def row_slice(j):
        return pl.ds(pl.multiple_of(j * block, block), block)

    def keys_of(back, tile):
        place = pl.ds(tile * TILE, TILE)
        key = own_ref[0, place, :] if back == 0 else kv[back - 1, 0, place, :]
        return jnp.concatenate([key, key_marks[back, place, :]], axis=1)

    def values_of(back, tile):
        place = pl.ds(tile * TILE, TILE)
        value = own_ref[1, place, :] if back == 0 else kv[back - 1, 1, place, :]
        return jnp.concatenate([value, jnp.ones((TILE, LANES), jnp.bfloat16)], axis=1)

    def score_tile(j, back, tile, column):
        query = jnp.concatenate([q_ref[row_slice(j), :], query_marks[row_slice(j), :]], axis=1)
        found = lax.dot_general(
            query, keys_of(back, tile), (((1,), (1,)), ((), ())), preferred_element_type=jnp.float32
        )
        if back == 0:
            token = lax.shift_right_logical(lax.broadcasted_iota(jnp.int32, (block, TILE), 0), heads.bit_length() - 1)
            key = lax.broadcasted_iota(jnp.int32, (block, TILE), 1)
            found = jnp.where(key - token <= j * chunk - tile * TILE, found, FAR)
        scores[:, column * TILE:(column + 1) * TILE] = found
        return jnp.maximum(found[:, :LANES], found[:, LANES:])

    def attend(j, parts, first):
        here = row_slice(j)
        peak = None
        for column, (back, tile) in enumerate(parts):
            top = score_tile(j, back, tile, column)
            peak = top if peak is None else jnp.maximum(peak, top)
        peak = jnp.max(peak, axis=1, keepdims=True)
        if first:
            peak = jnp.broadcast_to(peak, (block, LANES))
            summed = None
        else:
            before = peaks[here, :]
            peak = jnp.maximum(before, peak)
            shrink = jnp.exp2((before - peak) * exponent)
            summed = running[here, :] * jnp.concatenate([shrink, shrink], axis=1)
        wide = jnp.concatenate([peak, peak], axis=1)
        for column, (back, tile) in enumerate(parts):
            weight = jnp.exp2((scores[:, column * TILE:(column + 1) * TILE] - wide) * exponent)
            term = jnp.dot(
                weight.astype(jnp.bfloat16), values_of(back, tile), preferred_element_type=jnp.float32
            )
            summed = term if summed is None else summed + term
        return peak, summed

    def keep(j, parts, first):
        peak, summed = attend(j, parts, first)
        peaks[row_slice(j), :] = peak
        running[row_slice(j), :] = summed

    def own_step(j, carry):
        keep(j, [(0, tile) for tile in range(tiles)], True)
        return carry

    lax.fori_loop(0, tp_size, own_step, 0)

    for part in range(2):
        landed(1, part)
        hop(kv.at[1], 2 - 2 * core, 2, part, mate).start()
        hop(kv.at[1], 3, 3, part, ahead).start()
    for part in range(2):
        landed(0, part)

    def near_step(j, carry):
        keep(j, [(1, tile) for tile in range(tiles)], False)
        return carry

    lax.fori_loop(0, tp_size, near_step, 0)

    for part in range(2):
        landed(3, part)

        @pl.when(core == 1)
        def _():
            hop(kv.at[3], 2, 4, part, mate).start()

    for part in range(2):
        landed(2, part)

    def home(j, step):
        return pltpu.make_async_remote_copy(
            src_ref=outgoing.at[j],
            dst_ref=out_ref.at[pl.ds(head_place * heads, heads)],
            send_sem=out_send.at[step],
            recv_sem=out_recv.at[step],
            device_id=(span, j),
            device_id_type=MESH,
        )

    stay = pltpu.make_async_copy(
        outgoing.at[head_place], out_ref.at[pl.ds(head_place * heads, heads)], own_sem
    )

    def last_step(step, carry):
        j = lax.rem(head_place + 1 + step, tp_size)
        parts = [(back, tile) for back in (2, 3, 4) for tile in range(tiles)]
        _, summed = attend(j, parts, False)
        finished[...] = summed[:, :LANES] / summed[:, LANES:]
        for head in range(heads):
            outgoing[j, head] = finished[pl.ds(head, chunk, stride=heads), :].astype(jnp.bfloat16)

        @pl.when(step < tp_size - 1)
        def _():
            home(j, step).start()

        @pl.when(step == tp_size - 1)
        def _():
            stay.start()

        return carry

    lax.fori_loop(0, tp_size, last_step, 0)

    stay.wait()
    for step in range(tp_size - 1):
        home(lax.rem(head_place + 1 + step, tp_size), step).wait()
    for part in range(2):
        hop(own_ref, 1, 1, part, ahead).wait_send()
        hop(kv.at[1], 2 - 2 * core, 2, part, mate).wait_send()
        hop(kv.at[1], 3, 3, part, ahead).wait_send()

        @pl.when(core == 0)
        def _():
            hop(own_ref, 0, 0, part, mate).wait_send()

        @pl.when(core == 1)
        def _():
            hop(kv.at[3], 2, 4, part, mate).wait_send()


def per_device(queries, key_rows, value_rows, doc_ids, plan):
    rows, heads, dim = queries.shape
    tp_size = lax.axis_size("tp")
    chunk = rows // tp_size
    block = chunk * heads
    exponent = dim ** (-0.5) * 1.4426950408889634
    flat = queries.reshape(rows * heads, dim)
    own = jnp.stack([key_rows[:, 0], value_rows[:, 0]], 0)
    docs = doc_ids.reshape(-1, LANES)
    bf16, f32 = jnp.bfloat16, jnp.float32
    return pl.pallas_call(
        functools.partial(kernel, exponent),
        out_shape=jax.ShapeDtypeStruct((heads * tp_size, chunk, dim), bf16),
        in_specs=[pl.BlockSpec(memory_space=pltpu.VMEM)] * 3,
        out_specs=pl.BlockSpec(memory_space=pl.ANY),
        scratch_shapes=[
            pltpu.VMEM((4, 2, rows, dim), bf16),
            pltpu.VMEM((5, rows, LANES), bf16),
            pltpu.VMEM((rows * heads, LANES), bf16),
            pltpu.VMEM((block, 3 * rows), f32),
            pltpu.VMEM((rows * heads, LANES), f32),
            pltpu.VMEM((rows * heads, 2 * LANES), f32),
            pltpu.VMEM((block, dim), f32),
            pltpu.VMEM((tp_size, heads, chunk, dim), bf16),
            pltpu.SemaphoreType.DMA((5, 2)),
            pltpu.SemaphoreType.DMA((4, 2)),
            pltpu.SemaphoreType.DMA((tp_size - 1,)),
            pltpu.SemaphoreType.DMA((tp_size - 1,)),
            pltpu.SemaphoreType.DMA,
        ],
        compiler_params=pltpu.CompilerParams(
            collective_id=0, has_side_effects=True, vmem_limit_bytes=48 << 20
        ),
        cost_estimate=pl.CostEstimate(
            flops=4 * block * tp_size * 5 * rows * dim, bytes_accessed=8 * rows * heads * dim,
            transcendentals=block * tp_size * 5 * rows,
        ),
    )(flat, own, docs)


def solution(mesh):
    placed = (P("ctx", "tp", None), P("ctx", "tp", None), P("ctx", "tp", None), P(), P(None, "ctx"))
    return jax.shard_map(
        per_device,
        mesh=mesh,
        in_specs=placed,
        out_specs=P(None, ("ctx", "tp"), None),
        check_vma=False,
    )
```

```python
import functools

import jax
import jax.numpy as jnp
from jax import lax
from jax.experimental import pallas as pl
from jax.experimental.pallas import tpu as pltpu
from jax.sharding import PartitionSpec as P

MESH = pl.DeviceIdType.MESH
FAR = -1e30
TURNS = ((2, 1), (1, 1), (3, 0), (3, 1), (1, 0), (0, 1), (2, 0), (0, 0))
TILE = 256
LANES = 128


def packed(turns):
    return (
        sum(x << (2 * step) for step, (x, _) in enumerate(turns)),
        sum(y << step for step, (_, y) in enumerate(turns)),
    )


def kernel(exponent, q_hbm, k_hbm, v_hbm, docs_hbm, out_ref, q_ref, docs_ref, kv, key_marks, query_marks, scores_a, scores_b, tops_a, tops_b, peaks, running,
           finished, outgoing, kv_send, kv_recv, out_send, out_recv, load_sem, turn_sem):
    rows = k_hbm.shape[0]
    tp_size = outgoing.shape[0]
    heads = outgoing.shape[1]
    chunk = outgoing.shape[2]
    block = chunk * heads
    spans = lax.axis_size("ctx")
    doc_rows = rows // LANES
    tiles = rows // TILE
    span = lax.axis_index("ctx")
    head_place = lax.axis_index("tp")
    core = lax.rem(span, 2)
    mate = span + 1 - 2 * core
    ahead = lax.rem(span + 2 - core, spans)

    own_slot = 4
    own = kv.at[:, pl.ds(own_slot * rows, rows), :]
    loads = [
        pltpu.make_async_copy(source, target, load_sem.at[place])
        for place, (source, target) in enumerate(
            ((k_hbm, own.at[0]), (v_hbm, own.at[1]), (docs_hbm, docs_ref), (q_hbm, q_ref))
        )
    ]
    for load in loads:
        load.start()

    barrier = pltpu.get_barrier_semaphore()
    even, odd = core == 0, core == 1

    def greet(other):
        pl.semaphore_signal(
            barrier, inc=1, device_id=(lax.rem(other + spans, spans), head_place), device_id_type=MESH
        )

    def when(side, *acts):
        @pl.when(side)
        def _():
            for act in acts:
                act()

    greet(mate)
    greet(span + 2 - core)
    when(even, lambda: greet(span - 1), lambda: greet(span - 2))
    for step in range(1, tp_size):
        pl.semaphore_signal(
            barrier, inc=1, device_id=(span, lax.rem(head_place + step, tp_size)), device_id_type=MESH
        )
    pl.semaphore_wait(barrier, tp_size + 1 + 2 * (1 - core))

    for back in range(1, 5):

        @pl.when(span < back)
        def _():
            kv[:, (back - 1) * rows:back * rows, :] = jnp.zeros((2, rows, kv.shape[2]), kv.dtype)

    edge = kv.shape[1] - 5 * rows
    kv[:, 5 * rows:, :] = jnp.zeros((2, edge, kv.shape[2]), kv.dtype)
    key_marks[5 * rows:, :] = jnp.zeros((edge, LANES), key_marks.dtype)

    def slot_of(slot):
        return kv.at[:, pl.ds(slot * rows, rows), :]

    def hop(source, slot, kind, device):
        return pltpu.make_async_remote_copy(
            src_ref=slot_of(source),
            dst_ref=slot_of(slot),
            send_sem=kv_send.at[kind],
            recv_sem=kv_recv.at[slot],
            device_id=(device, head_place),
            device_id_type=MESH,
        )

    follows, leads = span + 2 - core < spans, span >= 2
    to_mate = hop(own_slot, 0, 0, mate), even
    to_ahead = hop(own_slot, 1 - core, 1, ahead), follows
    first_to_mate = hop(0, 1, 2, mate), even & leads
    first_to_ahead = hop(0, 2, 3, ahead), even & leads & follows
    second_to_mate = hop(1, 2, 4, mate), even & leads
    second_to_ahead = hop(1, 3, 5, ahead), even & leads & follows
    third_to_mate = hop(2, 3, 6, mate), even & (span >= 4)

    def go(task, side=None):
        copy, allowed = task
        pl.when(allowed if side is None else allowed & side)(copy.start)

    def landed(slot):
        pl.when(span > slot)(hop(own_slot, slot, 0, mate).wait_recv)

    for load in loads[:2]:
        load.wait()
    go(to_mate)
    go(to_ahead, odd)
    loads[2].wait()

    def mark(step, carry):
        for back in range(5):
            place = lax.rem(span + spans - back, spans) * doc_rows + step
            docs = docs_ref[pl.ds(place, 1), :]
            hit = lax.broadcasted_iota(jnp.int32, (LANES, LANES), 0) == docs
            turned = jnp.where(hit, 1.0, 0.0).astype(jnp.float32).T
            at = pl.multiple_of((back + 4) % 5 * rows + step * LANES, LANES)
            key_marks[pl.ds(at, LANES), :] = turned.astype(jnp.bfloat16)
            if back == 0:
                miss = (1.0 - turned) * FAR
                wide = jnp.broadcast_to(miss[:, None, :], (LANES, heads, LANES)).reshape(LANES * heads, LANES)
                at = pl.multiple_of(step * LANES * heads, LANES * heads)
                query_marks[pl.ds(at, LANES * heads), :] = wide.astype(jnp.bfloat16)
        return carry

    lax.fori_loop(0, doc_rows, mark, 0)
    loads[3].wait()

    def row_slice(j):
        return pl.ds(pl.multiple_of(j * block, block), block)

    def keys_of(at, count):
        place = pl.ds(at, count)
        return jnp.concatenate([kv[0, place, :], key_marks[place, :]], axis=1)

    def values_of(at, count):
        return jnp.concatenate([kv[1, pl.ds(at, count), :], jnp.ones((count, LANES), jnp.bfloat16)], axis=1)

    def parts_of(j, slots, window):
        parts = [(slot * rows + tile * TILE, TILE, False) for slot in slots for tile in range(tiles)]
        if window:
            start = (own_slot - 1) * rows + j * chunk
            for tile in range(tiles):
                parts.append((pl.multiple_of(start + tile * TILE, 32), TILE, False))
            parts.append((pl.multiple_of(start + rows, 32), LANES, True))
        return parts

    def score(j, kind, scores, tops):
        query = jnp.concatenate([q_ref[row_slice(j), :], query_marks[row_slice(j), :]], axis=1)
        peak = None
        column = 0
        for at, count, diagonal in parts_of(j, *kind):
            found = lax.dot_general(
                query, keys_of(at, count), (((1,), (1,)), ((), ())), preferred_element_type=jnp.float32
            )
            if diagonal:
                token = lax.shift_right_logical(
                    lax.broadcasted_iota(jnp.int32, (block, count), 0), heads.bit_length() - 1
                )
                key = lax.broadcasted_iota(jnp.int32, (block, count), 1)
                found = jnp.where(key <= token, found, FAR)
            scores[:, column:column + count] = found
            for lane in range(0, count, LANES):
                top = found[:, lane:lane + LANES]
                peak = top if peak is None else jnp.maximum(peak, top)
            column += count
        tops[...] = peak

    def weigh(j, kind, scores, tops, first):
        here = row_slice(j)
        peak = jnp.max(tops[...], axis=1, keepdims=True)
        if first:
            peak = jnp.broadcast_to(peak, (block, LANES))
            summed = None
        else:
            before = peaks[here, :]
            peak = jnp.maximum(before, peak)
            shrink = jnp.exp2((before - peak) * exponent)
            summed = running[here, :] * jnp.concatenate([shrink, shrink], axis=1)
        wide = jnp.concatenate([peak, peak], axis=1)
        column = 0
        for at, count, _ in parts_of(j, *kind):
            weight = jnp.exp2((scores[:, column:column + count] - wide[:, :count]) * exponent)
            column += count
            term = jnp.dot(weight.astype(jnp.bfloat16), values_of(at, count), preferred_element_type=jnp.float32)
            summed = term if summed is None else summed + term
        return peak, summed

    def keep(j, kind, scores, tops, first):
        peak, summed = weigh(j, kind, scores, tops, first)
        peaks[row_slice(j), :] = peak
        running[row_slice(j), :] = summed

    def sweep(order, kind, settle, after, hooks=()):
        def pair(place, carry):
            for when, act in hooks:
                pl.when(place == when)(act)
            for side in range(2):
                step = 2 * place + side
                score(order(step + 1), kind, *banks[1 - side])
                settle(step, order(step), *banks[side])
            return carry

        last = tp_size // 2 - 1
        lax.fori_loop(0, last, pair, 0)
        for when, act in hooks:
            if when == last:
                act()
        score(order(tp_size - 1), kind, *banks[1])
        settle(tp_size - 2, order(tp_size - 2), *banks[0])
        after()
        settle(tp_size - 1, order(tp_size - 1), *banks[1])

    banks = ((scores_a, tops_a), (scores_b, tops_b))
    near, second, third = ((0,), False), ((1,), False), ((2,), False)
    rest, window = ((2,), True), ((), True)

    def straight(step):
        return step

    turn_x, turn_y = packed(TURNS)

    def turned(step):
        x = lax.rem(head_place // 2 + lax.rem(lax.shift_right_logical(jnp.int32(turn_x), jnp.int32(2 * step)), 4), tp_size // 2)
        y = lax.rem(head_place + lax.shift_right_logical(jnp.int32(turn_y), jnp.int32(step)), 2)
        return 2 * x + y

    def hand_over():
        pl.when(follows)(to_ahead[0].wait_send)
        pl.semaphore_signal(turn_sem, inc=1, device_id=(mate, head_place), device_id_type=MESH)

    def enter_second():
        when(odd, lambda: landed(1))
        score(straight(0), second, *banks[0])

    def enter_third():
        when(even, lambda: score(straight(0), third, *banks[0]))
        when(odd, lambda: landed(2), lambda: landed(3), lambda: score(turned(0), rest, *banks[0]))

    def enter_window():
        landed(3)
        score(turned(0), window, *banks[0])

    def home(j, step):
        return pltpu.make_async_remote_copy(
            src_ref=outgoing.at[j],
            dst_ref=out_ref.at[pl.ds(head_place * heads, heads)],
            send_sem=out_send.at[step],
            recv_sem=out_recv.at[step],
            device_id=(span, j),
            device_id_type=MESH,
        )

    stay = pltpu.make_async_copy(
        outgoing.at[head_place], out_ref.at[pl.ds(head_place * heads, heads)], load_sem.at[0]
    )

    def finish(kind, step, j, scores, tops):
        _, summed = weigh(j, kind, scores, tops, False)
        finished[...] = summed[:, :LANES] / summed[:, LANES:]
        for head in range(heads):
            outgoing[j, head] = finished[pl.ds(head, chunk, stride=heads), :].astype(jnp.bfloat16)
        if isinstance(step, int) and step == tp_size - 1:
            stay.start()
        else:
            home(j, step).start()

    when(even, lambda: pl.semaphore_wait(turn_sem, 1), lambda: go(to_ahead))
    landed(0)
    go(first_to_mate)
    score(straight(0), near, *banks[0])
    sweep(
        straight, near, lambda step, j, *bank: keep(j, near, *bank, True), enter_second,
        (
            (1, lambda: when(odd, hand_over)),
            (1, lambda: go(first_to_ahead)),
            (3, lambda: when(even, lambda: landed(1))),
            (3, lambda: go(second_to_mate)),
        ),
    )
    sweep(
        straight, second, lambda step, j, *bank: keep(j, second, *bank, False), enter_third,
        (
            (0, lambda: go(second_to_ahead)),
            (2, lambda: when(even, lambda: landed(2))),
            (2, lambda: go(third_to_mate)),
        ),
    )

    @pl.when(even)
    def _():
        sweep(straight, third, lambda step, j, *bank: keep(j, third, *bank, False), enter_window)
        sweep(turned, window, functools.partial(finish, window), lambda: None)

    @pl.when(odd)
    def _():
        sweep(turned, rest, functools.partial(finish, rest), lambda: None)

    stay.wait()
    for step in range(tp_size - 1):
        home(turned(step), step).wait()
    pl.when(follows & even)(to_ahead[0].wait_send)
    for copy, allowed in (
        to_mate, first_to_mate, first_to_ahead, second_to_mate, second_to_ahead, third_to_mate
    ):
        pl.when(allowed)(copy.wait_send)


def per_device(queries, key_rows, value_rows, doc_ids, plan):
    rows, heads, dim = queries.shape
    tp_size = lax.axis_size("tp")
    chunk = rows // tp_size
    block = chunk * heads
    exponent = dim ** (-0.5) * 1.4426950408889634
    flat = queries.reshape(rows * heads, dim)
    own = key_rows.reshape(rows, dim), value_rows.reshape(rows, dim)
    docs = doc_ids.reshape(-1, LANES)
    bf16, f32 = jnp.bfloat16, jnp.float32
    return pl.pallas_call(
        functools.partial(kernel, exponent),
        out_shape=jax.ShapeDtypeStruct((heads * tp_size, chunk, dim), bf16),
        in_specs=[pl.BlockSpec(memory_space=pltpu.HBM)] * 4,
        out_specs=pl.BlockSpec(memory_space=pl.ANY),
        scratch_shapes=[
            pltpu.VMEM((rows * heads, dim), bf16),
            pltpu.VMEM(docs.shape, jnp.int32),
            pltpu.VMEM((2, 5 * rows + LANES - chunk, dim), bf16),
            pltpu.VMEM((5 * rows + LANES - chunk, LANES), bf16),
            pltpu.VMEM((rows * heads, LANES), bf16),
            pltpu.VMEM((block, 2 * rows + LANES), f32),
            pltpu.VMEM((block, 2 * rows + LANES), f32),
            pltpu.VMEM((block, LANES), f32),
            pltpu.VMEM((block, LANES), f32),
            pltpu.VMEM((rows * heads, LANES), f32),
            pltpu.VMEM((rows * heads, 2 * LANES), f32),
            pltpu.VMEM((block, dim), f32),
            pltpu.VMEM((tp_size, heads, chunk, dim), bf16),
            pltpu.SemaphoreType.DMA((7,)),
            pltpu.SemaphoreType.DMA((4,)),
            pltpu.SemaphoreType.DMA((tp_size - 1,)),
            pltpu.SemaphoreType.DMA((tp_size - 1,)),
            pltpu.SemaphoreType.DMA((4,)),
            pltpu.SemaphoreType.REGULAR,
        ],
        compiler_params=pltpu.CompilerParams(
            collective_id=0, has_side_effects=True, vmem_limit_bytes=62 << 20
        ),
        cost_estimate=pl.CostEstimate(
            flops=4 * block * tp_size * 5 * rows * dim, bytes_accessed=8 * rows * heads * dim,
            transcendentals=block * tp_size * 5 * rows,
        ),
    )(flat, *own, docs)


def solution(mesh):
    placed = (P("ctx", "tp", None), P("ctx", "tp", None), P("ctx", "tp", None), P(), P(None, "ctx"))
    return jax.shard_map(
        per_device,
        mesh=mesh,
        in_specs=placed,
        out_specs=P(None, ("ctx", "tp"), None),
        check_vma=False,
    )
```

```python
import functools

import jax
import jax.numpy as jnp
from jax import lax
from jax.experimental import pallas as pl
from jax.experimental.pallas import tpu as pltpu
from jax.sharding import PartitionSpec as P

MESH = pl.DeviceIdType.MESH
FAR = -1e30
TURNS = ((2, 1), (1, 1), (3, 0), (3, 1), (1, 0), (0, 1), (2, 0), (0, 0))
TILE = 256
LANES = 128


def packed(turns):
    return (
        sum(x << (2 * step) for step, (x, _) in enumerate(turns)),
        sum(y << step for step, (_, y) in enumerate(turns)),
    )


def kernel(exponent, q_hbm, k_hbm, v_hbm, docs_hbm, out_ref, q_ref, docs_ref, kv, key_marks, query_marks, scores_a, scores_b, tops_a, tops_b, peaks, running,
           finished, outgoing, kv_send, kv_recv, out_send, out_recv, load_sem, turn_sem):
    rows = k_hbm.shape[0]
    tp_size = outgoing.shape[0]
    heads = outgoing.shape[1]
    chunk = outgoing.shape[2]
    block = chunk * heads
    spans = lax.axis_size("ctx")
    doc_rows = rows // LANES
    tiles = rows // TILE
    span = lax.axis_index("ctx")
    head_place = lax.axis_index("tp")
    core = lax.rem(span, 2)
    mate = span + 1 - 2 * core
    ahead = lax.rem(span + 2 - core, spans)

    own_slot = 4
    own = kv.at[:, pl.ds(own_slot * rows, rows), :]
    loads = [
        pltpu.make_async_copy(source, target, load_sem.at[place])
        for place, (source, target) in enumerate(
            ((k_hbm, own.at[0]), (v_hbm, own.at[1]), (docs_hbm, docs_ref), (q_hbm, q_ref))
        )
    ]
    for load in loads:
        load.start()

    barrier = pltpu.get_barrier_semaphore()
    even, odd = core == 0, core == 1

    def greet(other):
        pl.semaphore_signal(
            barrier, inc=1, device_id=(lax.rem(other + spans, spans), head_place), device_id_type=MESH
        )

    def when(side, *acts):
        @pl.when(side)
        def _():
            for act in acts:
                act()

    greet(mate)
    greet(span + 2 - core)
    when(even, lambda: greet(span - 1), lambda: greet(span - 2), lambda: greet(span + 3))
    when(odd, lambda: greet(span - 3))
    for step in range(1, tp_size):
        pl.semaphore_signal(
            barrier, inc=1, device_id=(span, lax.rem(head_place + step, tp_size)), device_id_type=MESH
        )
    pl.semaphore_wait(barrier, tp_size + 2 + 2 * (1 - core))

    for back in range(1, 5):

        @pl.when(span < back)
        def _():
            kv[:, (back - 1) * rows:back * rows, :] = jnp.zeros((2, rows, kv.shape[2]), kv.dtype)

    edge = kv.shape[1] - 5 * rows
    kv[:, 5 * rows:, :] = jnp.zeros((2, edge, kv.shape[2]), kv.dtype)
    key_marks[5 * rows:, :] = jnp.zeros((edge, LANES), key_marks.dtype)

    def slot_of(slot):
        return kv.at[:, pl.ds(slot * rows, rows), :]

    def hop(source, slot, kind, device):
        return pltpu.make_async_remote_copy(
            src_ref=slot_of(source),
            dst_ref=slot_of(slot),
            send_sem=kv_send.at[kind],
            recv_sem=kv_recv.at[slot],
            device_id=(device, head_place),
            device_id_type=MESH,
        )

    follows, leads = span + 2 - core < spans, span >= 2
    to_mate = hop(own_slot, 0, 0, mate), even
    to_ahead = hop(own_slot, 1 - core, 1, ahead), follows
    first_to_mate = hop(0, 1, 2, mate), even & leads
    first_to_ahead = hop(0, 3, 3, lax.rem(span + 3, spans)), even & leads & (span + 3 < spans)
    second_to_mate = hop(1, 2, 4, mate), even & leads
    second_to_ahead = hop(1, 3, 5, ahead), even & leads & follows
    third_to_mate = hop(3, 2, 6, mate), odd & (span >= 5)

    def go(task, side=None):
        copy, allowed = task
        pl.when(allowed if side is None else allowed & side)(copy.start)

    def landed(slot):
        pl.when(span > slot)(hop(own_slot, slot, 0, mate).wait_recv)

    for load in loads[:2]:
        load.wait()
    go(to_mate)
    go(to_ahead, odd)
    loads[2].wait()

    def mark(step, carry):
        for back in range(5):
            place = lax.rem(span + spans - back, spans) * doc_rows + step
            docs = docs_ref[pl.ds(place, 1), :]
            hit = lax.broadcasted_iota(jnp.int32, (LANES, LANES), 0) == docs
            turned = jnp.where(hit, 1.0, 0.0).astype(jnp.float32).T
            at = pl.multiple_of((back + 4) % 5 * rows + step * LANES, LANES)
            key_marks[pl.ds(at, LANES), :] = turned.astype(jnp.bfloat16)
            if back == 0:
                miss = (1.0 - turned) * FAR
                wide = jnp.broadcast_to(miss[:, None, :], (LANES, heads, LANES)).reshape(LANES * heads, LANES)
                at = pl.multiple_of(step * LANES * heads, LANES * heads)
                query_marks[pl.ds(at, LANES * heads), :] = wide.astype(jnp.bfloat16)
        return carry

    lax.fori_loop(0, doc_rows, mark, 0)
    loads[3].wait()

    def row_slice(j):
        return pl.ds(pl.multiple_of(j * block, block), block)

    def keys_of(at, count):
        place = pl.ds(at, count)
        return jnp.concatenate([kv[0, place, :], key_marks[place, :]], axis=1)

    def values_of(at, count):
        return jnp.concatenate([kv[1, pl.ds(at, count), :], jnp.ones((count, LANES), jnp.bfloat16)], axis=1)

    def parts_of(j, slots, window):
        parts = [(slot * rows + tile * TILE, TILE, None) for slot in slots for tile in range(tiles)]
        if window == "shifted":
            start = (own_slot - 1) * rows + j * chunk
            for tile in range(tiles):
                parts.append((pl.multiple_of(start + tile * TILE, 32), TILE, None))
            parts.append((pl.multiple_of(start + rows, 32), LANES, 0))
        elif window == "own":
            for tile in range(-(-(j + 1) * chunk // TILE)):
                reach = j * chunk - tile * TILE
                parts.append((own_slot * rows + tile * TILE, TILE, reach if reach < TILE - 1 else None))
        return parts

    def score(j, kind, scores, tops):
        query = jnp.concatenate([q_ref[row_slice(j), :], query_marks[row_slice(j), :]], axis=1)
        peak = None
        column = 0
        for at, count, reach in parts_of(j, *kind):
            found = lax.dot_general(
                query, keys_of(at, count), (((1,), (1,)), ((), ())), preferred_element_type=jnp.float32
            )
            if reach is not None:
                token = lax.shift_right_logical(
                    lax.broadcasted_iota(jnp.int32, (block, count), 0), heads.bit_length() - 1
                )
                key = lax.broadcasted_iota(jnp.int32, (block, count), 1)
                found = jnp.where(key - token <= reach, found, FAR)
            scores[:, column:column + count] = found
            for lane in range(0, count, LANES):
                top = found[:, lane:lane + LANES]
                peak = top if peak is None else jnp.maximum(peak, top)
            column += count
        tops[...] = peak

    def weigh(j, kind, scores, tops, first):
        here = row_slice(j)
        peak = jnp.max(tops[...], axis=1, keepdims=True)
        if first:
            peak = jnp.broadcast_to(peak, (block, LANES))
            summed = None
        else:
            before = peaks[here, :]
            peak = jnp.maximum(before, peak)
            shrink = jnp.exp2((before - peak) * exponent)
            summed = running[here, :] * jnp.concatenate([shrink, shrink], axis=1)
        wide = jnp.concatenate([peak, peak], axis=1)
        column = 0
        for at, count, _ in parts_of(j, *kind):
            weight = jnp.exp2((scores[:, column:column + count] - wide[:, :count]) * exponent)
            column += count
            term = jnp.dot(weight.astype(jnp.bfloat16), values_of(at, count), preferred_element_type=jnp.float32)
            summed = term if summed is None else summed + term
        return peak, summed

    def keep(j, kind, scores, tops, first):
        peak, summed = weigh(j, kind, scores, tops, first)
        peaks[row_slice(j), :] = peak
        running[row_slice(j), :] = summed

    def sweep(order, kind, settle, after, hooks=()):
        def pair(place, carry):
            for when, act in hooks:
                pl.when(place == when)(act)
            for side in range(2):
                step = 2 * place + side
                score(order(step + 1), kind, *banks[1 - side])
                settle(step, order(step), *banks[side])
            return carry

        last = tp_size // 2 - 1
        lax.fori_loop(0, last, pair, 0)
        for when, act in hooks:
            if when == last:
                act()
        score(order(tp_size - 1), kind, *banks[1])
        settle(tp_size - 2, order(tp_size - 2), *banks[0])
        after()
        settle(tp_size - 1, order(tp_size - 1), *banks[1])

    banks = ((scores_a, tops_a), (scores_b, tops_b))
    own_part, near, second = ((), "own"), ((0,), ""), ((1,), "")
    last_even, last_odd = ((2, 3), ""), ((2,), "shifted")

    def straight(step):
        return step

    turn_x, turn_y = packed(TURNS)

    def turned(step):
        x = lax.rem(head_place // 2 + lax.rem(lax.shift_right_logical(jnp.int32(turn_x), jnp.int32(2 * step)), 4), tp_size // 2)
        y = lax.rem(head_place + lax.shift_right_logical(jnp.int32(turn_y), jnp.int32(step)), 2)
        return 2 * x + y

    def hand_over():
        pl.when(follows)(to_ahead[0].wait_send)
        pl.semaphore_signal(turn_sem, inc=1, device_id=(mate, head_place), device_id_type=MESH)

    def enter_second():
        when(odd, lambda: landed(1))
        score(straight(0), second, *banks[0])

    def enter_last():
        @pl.when(odd)
        def _():
            landed(3)
            go(third_to_mate)
            landed(2)
            score(turned(0), last_odd, *banks[0])

        @pl.when(even)
        def _():
            landed(2)
            landed(3)
            score(turned(0), last_even, *banks[0])

    def home(j, step):
        return pltpu.make_async_remote_copy(
            src_ref=outgoing.at[j],
            dst_ref=out_ref.at[pl.ds(head_place * heads, heads)],
            send_sem=out_send.at[step],
            recv_sem=out_recv.at[step],
            device_id=(span, j),
            device_id_type=MESH,
        )

    stay = pltpu.make_async_copy(
        outgoing.at[head_place], out_ref.at[pl.ds(head_place * heads, heads)], load_sem.at[0]
    )

    def finish(kind, step, j, scores, tops):
        _, summed = weigh(j, kind, scores, tops, False)
        finished[...] = summed[:, :LANES] / summed[:, LANES:]
        for head in range(heads):
            outgoing[j, head] = finished[pl.ds(head, chunk, stride=heads), :].astype(jnp.bfloat16)
        if isinstance(step, int) and step == tp_size - 1:
            stay.start()
        else:
            home(j, step).start()

    @pl.when(even)
    def _():
        score(0, own_part, *banks[0])
        for j in range(tp_size):
            if j == tp_size - 3:
                pl.semaphore_wait(turn_sem, 1)
                go(to_ahead)
            if j + 1 < tp_size:
                score(j + 1, own_part, *banks[(j + 1) % 2])
            keep(j, own_part, *banks[j % 2], True)

    @pl.when(odd)
    def _():
        peaks[...] = jnp.full(peaks.shape, FAR, peaks.dtype)
        running[...] = jnp.zeros(running.shape, running.dtype)

    landed(0)
    go(first_to_mate)
    score(straight(0), near, *banks[0])
    sweep(
        straight, near, lambda step, j, *bank: keep(j, near, *bank, False), enter_second,
        (
            (1, lambda: when(odd, hand_over)),
            (1, lambda: go(first_to_ahead)),
            (3, lambda: when(even, lambda: landed(1))),
            (3, lambda: go(second_to_mate)),
            (3, lambda: go(second_to_ahead)),
        ),
    )
    sweep(
        straight, second, lambda step, j, *bank: keep(j, second, *bank, False), enter_last
    )
    for side, kind in ((even, last_even), (odd, last_odd)):
        when(side, functools.partial(sweep, turned, kind, functools.partial(finish, kind), lambda: None))

    stay.wait()
    for step in range(tp_size - 1):
        home(turned(step), step).wait()
    pl.when(follows & even)(to_ahead[0].wait_send)
    for copy, allowed in (
        to_mate, first_to_mate, first_to_ahead, second_to_mate, second_to_ahead, third_to_mate
    ):
        pl.when(allowed)(copy.wait_send)


def move(parts, source, target, held, into_sem, out_sem):
    share = source.shape[0] // parts
    pieces = [pl.ds(part * share, share) for part in range(parts)]
    into = [pltpu.make_async_copy(source.at[p], held.at[p], into_sem.at[i]) for i, p in enumerate(pieces)]
    out = [pltpu.make_async_copy(held.at[p], target.at[p], out_sem.at[i]) for i, p in enumerate(pieces)]
    for copy in into:
        copy.start()
    for arrive, leave in zip(into, out):
        arrive.wait()
        leave.start()
    for copy in out:
        copy.wait()


def per_device(queries, key_rows, value_rows, doc_ids, plan):
    rows, heads, dim = queries.shape
    tp_size = lax.axis_size("tp")
    chunk = rows // tp_size
    block = chunk * heads
    exponent = dim ** (-0.5) * 1.4426950408889634
    flat = queries.reshape(rows * heads, dim)
    own = key_rows.reshape(rows, dim), value_rows.reshape(rows, dim)
    docs = doc_ids.reshape(-1, LANES)
    bf16, f32 = jnp.bfloat16, jnp.float32
    attended = pl.pallas_call(
        functools.partial(kernel, exponent),
        out_shape=jax.ShapeDtypeStruct((heads * tp_size, chunk, dim), bf16),
        in_specs=[pl.BlockSpec(memory_space=pltpu.HBM)] * 4,
        out_specs=pl.BlockSpec(memory_space=pl.ANY),
        scratch_shapes=[
            pltpu.VMEM((rows * heads, dim), bf16),
            pltpu.VMEM(docs.shape, jnp.int32),
            pltpu.VMEM((2, 5 * rows + LANES - chunk, dim), bf16),
            pltpu.VMEM((5 * rows + LANES - chunk, LANES), bf16),
            pltpu.VMEM((rows * heads, LANES), bf16),
            pltpu.VMEM((block, 2 * rows + LANES), f32),
            pltpu.VMEM((block, 2 * rows + LANES), f32),
            pltpu.VMEM((block, LANES), f32),
            pltpu.VMEM((block, LANES), f32),
            pltpu.VMEM((rows * heads, LANES), f32),
            pltpu.VMEM((rows * heads, 2 * LANES), f32),
            pltpu.VMEM((block, dim), f32),
            pltpu.VMEM((tp_size, heads, chunk, dim), bf16),
            pltpu.SemaphoreType.DMA((7,)),
            pltpu.SemaphoreType.DMA((4,)),
            pltpu.SemaphoreType.DMA((tp_size - 1,)),
            pltpu.SemaphoreType.DMA((tp_size - 1,)),
            pltpu.SemaphoreType.DMA((4,)),
            pltpu.SemaphoreType.REGULAR,
        ],
        compiler_params=pltpu.CompilerParams(
            collective_id=0, has_side_effects=True, vmem_limit_bytes=62 << 20
        ),
        cost_estimate=pl.CostEstimate(
            flops=4 * block * tp_size * 5 * rows * dim, bytes_accessed=8 * rows * heads * dim,
            transcendentals=block * tp_size * 5 * rows,
        ),
    )(flat, *own, docs)
    return pl.pallas_call(
        functools.partial(move, 4),
        out_shape=jax.ShapeDtypeStruct(attended.shape, bf16),
        in_specs=[pl.BlockSpec(memory_space=pltpu.HBM)],
        out_specs=pl.BlockSpec(memory_space=pltpu.HBM),
        scratch_shapes=[
            pltpu.VMEM(attended.shape, bf16),
            pltpu.SemaphoreType.DMA((4,)),
            pltpu.SemaphoreType.DMA((4,)),
        ],
        compiler_params=pltpu.CompilerParams(vmem_limit_bytes=62 << 20),
    )(attended)


def solution(mesh):
    placed = (P("ctx", "tp", None), P("ctx", "tp", None), P("ctx", "tp", None), P(), P(None, "ctx"))
    return jax.shard_map(
        per_device,
        mesh=mesh,
        in_specs=placed,
        out_specs=P(None, ("ctx", "tp"), None),
        check_vma=False,
    )
```

```python
import functools

import jax
import jax.numpy as jnp
from jax import lax
from jax.experimental import pallas as pl
from jax.experimental.pallas import tpu as pltpu
from jax.sharding import PartitionSpec as P

MESH = pl.DeviceIdType.MESH
FAR = -1e30
TURNS = ((2, 1), (1, 1), (3, 0), (3, 1), (1, 0), (0, 1), (2, 0), (0, 0))
TILE = 256
LANES = 128


def packed(turns):
    return (
        sum(x << (2 * step) for step, (x, _) in enumerate(turns)),
        sum(y << step for step, (_, y) in enumerate(turns)),
    )


def kernel(exponent, q_hbm, k_hbm, v_hbm, docs_hbm, out_ref, q_ref, docs_ref, kv, key_marks, query_marks, scores_a, scores_b, tops_a, tops_b, peaks, running,
           finished, outgoing, kv_send, kv_recv, out_send, out_recv, load_sem, turn_sem):
    rows = k_hbm.shape[0]
    tp_size = outgoing.shape[0]
    heads = outgoing.shape[1]
    chunk = outgoing.shape[2]
    block = chunk * heads
    spans = lax.axis_size("ctx")
    doc_rows = rows // LANES
    tiles = rows // TILE
    span = lax.axis_index("ctx")
    head_place = lax.axis_index("tp")
    core = lax.rem(span, 2)
    mate = span + 1 - 2 * core
    ahead = lax.rem(span + 2 - core, spans)

    own_slot = 4
    own = kv.at[:, pl.ds(own_slot * rows, rows), :]
    loads = [
        pltpu.make_async_copy(source, target, load_sem.at[place])
        for place, (source, target) in enumerate(
            ((k_hbm, own.at[0]), (v_hbm, own.at[1]), (docs_hbm, docs_ref), (q_hbm, q_ref))
        )
    ]
    for load in loads:
        load.start()

    barrier = pltpu.get_barrier_semaphore()
    even, odd = core == 0, core == 1

    def greet(other):
        pl.semaphore_signal(
            barrier, inc=1, device_id=(lax.rem(other + spans, spans), head_place), device_id_type=MESH
        )

    def when(side, *acts):
        @pl.when(side)
        def _():
            for act in acts:
                act()

    greet(mate)
    greet(span + 2 - core)
    when(even, lambda: greet(span - 1), lambda: greet(span - 2), lambda: greet(span + 3))
    when(odd, lambda: greet(span - 3))
    for step in range(1, tp_size):
        pl.semaphore_signal(
            barrier, inc=1, device_id=(span, lax.rem(head_place + step, tp_size)), device_id_type=MESH
        )
    pl.semaphore_wait(barrier, tp_size + 2 + 2 * (1 - core))

    for back in range(1, 5):

        @pl.when(span < back)
        def _():
            kv[:, (back - 1) * rows:back * rows, :] = jnp.zeros((2, rows, kv.shape[2]), kv.dtype)

    edge = kv.shape[1] - 5 * rows
    kv[:, 5 * rows:, :] = jnp.zeros((2, edge, kv.shape[2]), kv.dtype)
    key_marks[5 * rows:, :] = jnp.zeros((edge, LANES), key_marks.dtype)

    def slot_of(slot):
        return kv.at[:, pl.ds(slot * rows, rows), :]

    def hop(source, slot, kind, device):
        return pltpu.make_async_remote_copy(
            src_ref=slot_of(source),
            dst_ref=slot_of(slot),
            send_sem=kv_send.at[kind],
            recv_sem=kv_recv.at[slot],
            device_id=(device, head_place),
            device_id_type=MESH,
        )

    follows, leads = span + 2 - core < spans, span >= 2
    to_mate = hop(own_slot, 0, 0, mate), even
    to_ahead = hop(own_slot, 1 - core, 1, ahead), follows
    first_to_mate = hop(0, 1, 2, mate), even & leads
    first_to_ahead = hop(0, 3, 3, lax.rem(span + 3, spans)), even & leads & (span + 3 < spans)
    second_to_mate = hop(1, 2, 4, mate), even & leads
    second_to_ahead = hop(1, 3, 5, ahead), even & leads & follows
    third_to_mate = hop(3, 2, 6, mate), odd & (span >= 5)

    def go(task, side=None):
        copy, allowed = task
        pl.when(allowed if side is None else allowed & side)(copy.start)

    def landed(slot):
        pl.when(span > slot)(hop(own_slot, slot, 0, mate).wait_recv)

    for load in loads[:2]:
        load.wait()
    go(to_mate)
    go(to_ahead, odd)
    loads[2].wait()

    def mark(step, carry):
        for back in range(5):
            place = lax.rem(span + spans - back, spans) * doc_rows + step
            docs = docs_ref[pl.ds(place, 1), :]
            hit = lax.broadcasted_iota(jnp.int32, (LANES, LANES), 0) == docs
            turned = jnp.where(hit, 1.0, 0.0).astype(jnp.float32).T
            at = pl.multiple_of((back + 4) % 5 * rows + step * LANES, LANES)
            key_marks[pl.ds(at, LANES), :] = turned.astype(jnp.bfloat16)
            if back == 0:
                miss = (1.0 - turned) * FAR
                wide = jnp.broadcast_to(miss[:, None, :], (LANES, heads, LANES)).reshape(LANES * heads, LANES)
                at = pl.multiple_of(step * LANES * heads, LANES * heads)
                query_marks[pl.ds(at, LANES * heads), :] = wide.astype(jnp.bfloat16)
        return carry

    lax.fori_loop(0, doc_rows, mark, 0)
    loads[3].wait()

    def row_slice(j):
        return pl.ds(pl.multiple_of(j * block, block), block)

    def keys_of(at, count):
        place = pl.ds(at, count)
        return jnp.concatenate([kv[0, place, :], key_marks[place, :]], axis=1)

    def values_of(at, count):
        return jnp.concatenate([kv[1, pl.ds(at, count), :], jnp.ones((count, LANES), jnp.bfloat16)], axis=1)

    def parts_of(j, slots, window):
        parts = [(slot * rows + tile * TILE, TILE, None) for slot in slots for tile in range(tiles)]
        if window == "shifted":
            start = (own_slot - 1) * rows + j * chunk
            for tile in range(tiles):
                parts.append((pl.multiple_of(start + tile * TILE, 32), TILE, None))
            parts.append((pl.multiple_of(start + rows, 32), LANES, 0))
        elif window == "own":
            for tile in range(-(-(j + 1) * chunk // TILE)):
                reach = j * chunk - tile * TILE
                parts.append((own_slot * rows + tile * TILE, TILE, reach if reach < TILE - 1 else None))
        return parts

    def score(j, kind, scores, tops):
        query = jnp.concatenate([q_ref[row_slice(j), :], query_marks[row_slice(j), :]], axis=1)
        peak = None
        column = 0
        for at, count, reach in parts_of(j, *kind):
            found = lax.dot_general(
                query, keys_of(at, count), (((1,), (1,)), ((), ())), preferred_element_type=jnp.float32
            )
            if reach is not None:
                token = lax.shift_right_logical(
                    lax.broadcasted_iota(jnp.int32, (block, count), 0), heads.bit_length() - 1
                )
                key = lax.broadcasted_iota(jnp.int32, (block, count), 1)
                found = jnp.where(key - token <= reach, found, FAR)
            scores[:, column:column + count] = found
            for lane in range(0, count, LANES):
                top = found[:, lane:lane + LANES]
                peak = top if peak is None else jnp.maximum(peak, top)
            column += count
        tops[...] = peak

    def weigh(j, kind, scores, tops, first):
        here = row_slice(j)
        peak = jnp.max(tops[...], axis=1, keepdims=True)
        if first:
            peak = jnp.broadcast_to(peak, (block, LANES))
            summed = None
        else:
            before = peaks[here, :]
            peak = jnp.maximum(before, peak)
            shrink = jnp.exp2((before - peak) * exponent)
            summed = running[here, :] * jnp.concatenate([shrink, shrink], axis=1)
        wide = jnp.concatenate([peak, peak], axis=1)
        column = 0
        for at, count, _ in parts_of(j, *kind):
            weight = jnp.exp2((scores[:, column:column + count] - wide[:, :count]) * exponent)
            column += count
            term = jnp.dot(weight.astype(jnp.bfloat16), values_of(at, count), preferred_element_type=jnp.float32)
            summed = term if summed is None else summed + term
        return peak, summed

    def keep(j, kind, scores, tops, first):
        peak, summed = weigh(j, kind, scores, tops, first)
        peaks[row_slice(j), :] = peak
        running[row_slice(j), :] = summed

    def sweep(order, kind, settle, after, hooks=()):
        def pair(place, carry):
            for when, act in hooks:
                pl.when(place == when)(act)
            for side in range(2):
                step = 2 * place + side
                score(order(step + 1), kind, *banks[1 - side])
                settle(step, order(step), *banks[side])
            return carry

        last = tp_size // 2 - 1
        lax.fori_loop(0, last, pair, 0)
        for when, act in hooks:
            if when == last:
                act()
        score(order(tp_size - 1), kind, *banks[1])
        settle(tp_size - 2, order(tp_size - 2), *banks[0])
        after()
        settle(tp_size - 1, order(tp_size - 1), *banks[1])

    banks = ((scores_a, tops_a), (scores_b, tops_b))
    own_part, near, second = ((), "own"), ((0,), ""), ((1,), "")
    last_even, last_odd = ((2, 3), ""), ((2,), "shifted")

    def straight(step):
        return step

    turn_x, turn_y = packed(TURNS)

    def turned(step):
        right = lax.rem(lax.shift_right_logical(jnp.int32(turn_x), jnp.int32(2 * step)), 4)
        x = lax.rem(head_place // 2 + jnp.where(even, tp_size // 2 - right, right), tp_size // 2)
        y = lax.rem(head_place + lax.shift_right_logical(jnp.int32(turn_y), jnp.int32(step)), 2)
        return 2 * x + y

    def hand_over():
        pl.when(follows)(to_ahead[0].wait_send)
        pl.semaphore_signal(turn_sem, inc=1, device_id=(mate, head_place), device_id_type=MESH)

    def enter_second():
        when(odd, lambda: landed(1))
        score(straight(0), second, *banks[0])

    def enter_last():
        @pl.when(odd)
        def _():
            landed(3)
            go(third_to_mate)
            landed(2)
            score(turned(0), last_odd, *banks[0])

        @pl.when(even)
        def _():
            landed(2)
            landed(3)
            score(turned(0), last_even, *banks[0])

    def home(j, step):
        return pltpu.make_async_remote_copy(
            src_ref=outgoing.at[j],
            dst_ref=out_ref.at[pl.ds(head_place * heads, heads)],
            send_sem=out_send.at[step],
            recv_sem=out_recv.at[step],
            device_id=(span, j),
            device_id_type=MESH,
        )

    stay = pltpu.make_async_copy(
        outgoing.at[head_place], out_ref.at[pl.ds(head_place * heads, heads)], load_sem.at[0]
    )

    def finish(kind, step, j, scores, tops):
        _, summed = weigh(j, kind, scores, tops, False)
        finished[...] = summed[:, :LANES] / summed[:, LANES:]
        for head in range(heads):
            outgoing[j, head] = finished[pl.ds(head, chunk, stride=heads), :].astype(jnp.bfloat16)
        if isinstance(step, int) and step == tp_size - 1:
            stay.start()
        else:
            home(j, step).start()

    @pl.when(even)
    def _():
        score(0, own_part, *banks[0])
        for j in range(tp_size):
            if j == tp_size - 3:
                pl.semaphore_wait(turn_sem, 1)
                go(to_ahead)
            if j + 1 < tp_size:
                score(j + 1, own_part, *banks[(j + 1) % 2])
            keep(j, own_part, *banks[j % 2], True)

    @pl.when(odd)
    def _():
        peaks[...] = jnp.full(peaks.shape, FAR, peaks.dtype)
        running[...] = jnp.zeros(running.shape, running.dtype)

    landed(0)
    go(first_to_mate)
    score(straight(0), near, *banks[0])
    sweep(
        straight, near, lambda step, j, *bank: keep(j, near, *bank, False), enter_second,
        (
            (1, lambda: when(odd, hand_over)),
            (1, lambda: go(first_to_ahead)),
            (3, lambda: when(even, lambda: landed(1))),
            (3, lambda: go(second_to_mate)),
            (3, lambda: go(second_to_ahead)),
        ),
    )
    sweep(
        straight, second, lambda step, j, *bank: keep(j, second, *bank, False), enter_last
    )
    for side, kind in ((even, last_even), (odd, last_odd)):
        when(side, functools.partial(sweep, turned, kind, functools.partial(finish, kind), lambda: None))

    stay.wait()
    for step in range(tp_size - 1):
        home(turned(step), step).wait()
    pl.when(follows & even)(to_ahead[0].wait_send)
    for copy, allowed in (
        to_mate, first_to_mate, first_to_ahead, second_to_mate, second_to_ahead, third_to_mate
    ):
        pl.when(allowed)(copy.wait_send)


def move(parts, source, target, held, into_sem, out_sem):
    share = source.shape[0] // parts
    pieces = [pl.ds(part * share, share) for part in range(parts)]
    into = [pltpu.make_async_copy(source.at[p], held.at[p], into_sem.at[i]) for i, p in enumerate(pieces)]
    out = [pltpu.make_async_copy(held.at[p], target.at[p], out_sem.at[i]) for i, p in enumerate(pieces)]
    for copy in into:
        copy.start()
    for arrive, leave in zip(into, out):
        arrive.wait()
        leave.start()
    for copy in out:
        copy.wait()


def per_device(queries, key_rows, value_rows, doc_ids, plan):
    rows, heads, dim = queries.shape
    tp_size = lax.axis_size("tp")
    chunk = rows // tp_size
    block = chunk * heads
    exponent = dim ** (-0.5) * 1.4426950408889634
    flat = queries.reshape(rows * heads, dim)
    own = key_rows.reshape(rows, dim), value_rows.reshape(rows, dim)
    docs = doc_ids.reshape(-1, LANES)
    bf16, f32 = jnp.bfloat16, jnp.float32
    attended = pl.pallas_call(
        functools.partial(kernel, exponent),
        out_shape=jax.ShapeDtypeStruct((heads * tp_size, chunk, dim), bf16),
        in_specs=[pl.BlockSpec(memory_space=pltpu.HBM)] * 4,
        out_specs=pl.BlockSpec(memory_space=pl.ANY),
        scratch_shapes=[
            pltpu.VMEM((rows * heads, dim), bf16),
            pltpu.VMEM(docs.shape, jnp.int32),
            pltpu.VMEM((2, 5 * rows + LANES - chunk, dim), bf16),
            pltpu.VMEM((5 * rows + LANES - chunk, LANES), bf16),
            pltpu.VMEM((rows * heads, LANES), bf16),
            pltpu.VMEM((block, 2 * rows + LANES), f32),
            pltpu.VMEM((block, 2 * rows + LANES), f32),
            pltpu.VMEM((block, LANES), f32),
            pltpu.VMEM((block, LANES), f32),
            pltpu.VMEM((rows * heads, LANES), f32),
            pltpu.VMEM((rows * heads, 2 * LANES), f32),
            pltpu.VMEM((block, dim), f32),
            pltpu.VMEM((tp_size, heads, chunk, dim), bf16),
            pltpu.SemaphoreType.DMA((7,)),
            pltpu.SemaphoreType.DMA((4,)),
            pltpu.SemaphoreType.DMA((tp_size - 1,)),
            pltpu.SemaphoreType.DMA((tp_size - 1,)),
            pltpu.SemaphoreType.DMA((4,)),
            pltpu.SemaphoreType.REGULAR,
        ],
        compiler_params=pltpu.CompilerParams(
            collective_id=0, has_side_effects=True, vmem_limit_bytes=62 << 20
        ),
        cost_estimate=pl.CostEstimate(
            flops=4 * block * tp_size * 5 * rows * dim, bytes_accessed=8 * rows * heads * dim,
            transcendentals=block * tp_size * 5 * rows,
        ),
    )(flat, *own, docs)
    return pl.pallas_call(
        functools.partial(move, 4),
        out_shape=jax.ShapeDtypeStruct(attended.shape, bf16),
        in_specs=[pl.BlockSpec(memory_space=pltpu.HBM)],
        out_specs=pl.BlockSpec(memory_space=pltpu.HBM),
        scratch_shapes=[
            pltpu.VMEM(attended.shape, bf16),
            pltpu.SemaphoreType.DMA((4,)),
            pltpu.SemaphoreType.DMA((4,)),
        ],
        compiler_params=pltpu.CompilerParams(vmem_limit_bytes=62 << 20),
    )(attended)


def solution(mesh):
    placed = (P("ctx", "tp", None), P("ctx", "tp", None), P("ctx", "tp", None), P(), P(None, "ctx"))
    return jax.shard_map(
        per_device,
        mesh=mesh,
        in_specs=placed,
        out_specs=P(None, ("ctx", "tp"), None),
        check_vma=False,
    )
```
